32 devices in a mesh: seq: 8 (over z, x), head: 4 (over y, core).
Axes of the slice: x: 2, y: 2, z: 4, core: 2. Of those that a mesh axis runs over, the one named last changes fastest.
Arguments:
- stretch_queries: bfloat16 [1024, 8192], P(('seq', 'head')), may hold values from -40 to 40, as said below
- stretch_key_values: bfloat16 [1024, 2048], P(('seq', 'head')), may hold values from -6 to 6
- suffix_queries: bfloat16 [1024, 8192], P(('seq', 'head')), may hold values from -40 to 40, as said below
- suffix_key_values: bfloat16 [1024, 2048], P(('seq', 'head')), may hold values from -6 to 6
- prefix_key_values: bfloat16 [2048, 2048], P('seq', 'head'), may hold values from -40 to 40, as said below
- set_length: int32 [8], P('seq'), may hold values from 1 to 128, as said below
- passage_first_slot: int32 [8, 4], P('seq'), may hold values from 0 to 127, as said below
Outputs:
- stretch_out: bfloat16 [1024, 8192], P(('seq', 'head'))
- suffix_output: bfloat16 [1024, 8192], P(('seq', 'head'))
The draws below stay inside these ranges and needn't reach their ends.
Inputs may be any that keep to these rules, and one draw needn't show every extreme that they name: `set_length`: each set has from 1 to 128 live slots; at least one set is full. `passage_first_slot`: each row starts with 0 and never falls; in some set the last passage starts at slot 127. `stretch_queries`: entries of order one, some rows larger. `suffix_queries`: entries of order one, some rows larger. `prefix_key_values`: entries of order one, some rows larger.
All inputs are finite; a program needn't handle non-finite values.
Results may differ from the reference program's by a relative error of at most 0.0095.
Values may be sent and summed in bfloat16 or wider, within the bound.
No kernel may reach another device: no remote copies, remote signals or barrier semaphores. Data moves between devices by JAX's collectives and lax.ppermute only.
A program may use at most 64 MiB of HBM per device.

```python
import math
import jax
import jax.numpy as jnp
from jax import lax

QUERY_HEADS = 64
KEY_VALUE_HEADS = 8
HEAD_SIZE = 128
SET_SLOTS = 128
STRETCH_TOKENS = 1024
PREFIX_TOKENS = 2048
SUFFIX_SETS = 8
SUFFIX_SLOTS = 1024


def query_values(key, rows):
    return jnp.clip(jax.random.normal(key, (rows, QUERY_HEADS * HEAD_SIZE), jnp.float32), -6.0, 6.0)


def draw_stretch_queries(key, part):
    key = jax.random.fold_in(key, 1)
    value_rows = query_values(key, STRETCH_TOKENS)
    return value_rows.astype(jnp.bfloat16)


def draw_suffix_queries(key, part):
    key = jax.random.fold_in(key, 2)
    value_rows = query_values(key, SUFFIX_SLOTS)
    return value_rows.astype(jnp.bfloat16)


def draw_prefix_key_values(key, part):
    key = jax.random.fold_in(key, 3)
    value_rows = jnp.clip(jax.random.normal(key, (PREFIX_TOKENS, KEY_VALUE_HEADS, 2, HEAD_SIZE), jnp.float32), -6.0, 6.0)
    return value_rows.reshape(PREFIX_TOKENS, KEY_VALUE_HEADS * 2 * HEAD_SIZE).astype(jnp.bfloat16)


def draw_set_length(key, part):
    key = jax.random.fold_in(key, 4)
    first, second = jax.random.split(key)
    lengths = jax.random.randint(first, (SUFFIX_SETS,), 1, SET_SLOTS + 1, dtype=jnp.int32)
    full = jax.random.randint(second, (), 0, SUFFIX_SETS, dtype=jnp.int32)
    return jnp.where(jnp.arange(SUFFIX_SETS, dtype=jnp.int32) == full, SET_SLOTS, lengths).astype(jnp.int32)


def draw_passage_first_slot(key, part):
    key = jax.random.fold_in(key, 5)
    first, second = jax.random.split(key)
    inner = jnp.sort(jax.random.randint(first, (SUFFIX_SETS, 3), 1, SET_SLOTS, dtype=jnp.int32), axis=1)
    pick = jax.random.randint(second, (), 0, SUFFIX_SETS, dtype=jnp.int32)
    last = jnp.where(jnp.arange(SUFFIX_SETS, dtype=jnp.int32) == pick, SET_SLOTS - 1, inner[:, 2])
    starts = jnp.concatenate([jnp.zeros((SUFFIX_SETS, 1), jnp.int32), inner[:, :2], last[:, None]], axis=1)
    return starts.astype(jnp.int32)


def shard_levels(key, dims, cuts, low, high):
    def one(dim, blocks):
        heights = jax.random.uniform(jax.random.fold_in(jax.random.fold_in(key, 6), dim), (blocks,), jnp.float32, low / len(cuts), high / len(cuts))
        return jnp.repeat(jnp.exp(heights), dims[dim] // blocks).reshape((-1,) + (1,) * (len(dims) - dim - 1))

    factor_of = one(*cuts[0])
    for cut in cuts[1:]:
        factor_of = factor_of * one(*cut)
    return factor_of


def bell_draw(rng, dims, scale, bound, cuts=(), kind=jnp.bfloat16):
    array = jax.random.normal(rng, dims, jnp.float32) * scale
    if len(cuts) > 0:
        array = shard_levels(rng, dims, cuts, -0.22, 0.18) * array
    return jnp.clip(array, min=-bound, max=bound).astype(kind)


def setup_inputs(seed: int = 0) -> dict:
    arg_keys = jax.random.split(jax.random.key(seed), 8)
    stretch_queries = draw_stretch_queries(jax.random.fold_in(arg_keys[7], 71), 0)
    stretch_key_values = bell_draw(arg_keys[1], (STRETCH_TOKENS, KEY_VALUE_HEADS * 2 * HEAD_SIZE), 1.0, 6.0, ((0, 32),))
    suffix_queries = draw_suffix_queries(jax.random.fold_in(arg_keys[7], 71), 0)
    suffix_key_values = bell_draw(arg_keys[3], (SUFFIX_SLOTS, KEY_VALUE_HEADS * 2 * HEAD_SIZE), 1.0, 6.0, ((0, 32),))
    prefix_key_values = draw_prefix_key_values(jax.random.fold_in(arg_keys[7], 71), 0)
    set_length = draw_set_length(jax.random.fold_in(arg_keys[7], 71), 0)
    passage_first_slot = draw_passage_first_slot(jax.random.fold_in(arg_keys[7], 71), 0)
    return dict(stretch_queries=stretch_queries, stretch_key_values=stretch_key_values, suffix_queries=suffix_queries, suffix_key_values=suffix_key_values, prefix_key_values=prefix_key_values, set_length=set_length, passage_first_slot=passage_first_slot)


def attend(queries, keys, vals, mask):
    scores = jnp.einsum("rgd,kd->grk", queries.astype(jnp.float32), keys.astype(jnp.float32)) * (HEAD_SIZE ** -0.5)
    scores = jnp.where(mask[None], scores, -1e30)
    peak = jnp.max(scores, axis=-1, keepdims=True)
    weights = jnp.where(mask[None], jnp.exp(scores - peak), 0.0)
    total = jnp.sum(weights, axis=-1)
    rounded = lax.optimization_barrier(weights.astype(jnp.bfloat16)).astype(jnp.float32)
    acc = jnp.einsum("grk,kd->grd", rounded, vals.astype(jnp.float32))
    return acc / total[..., None]


def reference(stretch_queries, stretch_key_values, suffix_queries, suffix_key_values, prefix_key_values, set_length, passage_first_slot):
    query_group = QUERY_HEADS // KEY_VALUE_HEADS
    current_query = stretch_queries.reshape(STRETCH_TOKENS, KEY_VALUE_HEADS, query_group, HEAD_SIZE).transpose(1, 0, 2, 3)
    current_key_value = stretch_key_values.reshape(STRETCH_TOKENS, KEY_VALUE_HEADS, 2, HEAD_SIZE).transpose(1, 2, 0, 3)
    prefix_key_value = prefix_key_values.reshape(PREFIX_TOKENS, KEY_VALUE_HEADS, 2, HEAD_SIZE).transpose(1, 2, 0, 3)
    keys = jnp.concatenate([prefix_key_value[:, 0], current_key_value[:, 0]], axis=1)
    vals = jnp.concatenate([prefix_key_value[:, 1], current_key_value[:, 1]], axis=1)
    block = math.gcd(STRETCH_TOKENS, 512)
    key_index = jnp.arange(PREFIX_TOKENS + STRETCH_TOKENS, dtype=jnp.int32)

    def stretch_head(operands):
        q_head, k_head, v_head = operands

        def one_block(start):
            q_block = lax.dynamic_slice_in_dim(q_head, start, block, 0)
            q_pos = start + jnp.arange(block, dtype=jnp.int32)
            mask = (key_index[None, :] < PREFIX_TOKENS) | (key_index[None, :] - PREFIX_TOKENS <= q_pos[:, None])
            return attend(q_block, k_head, v_head, mask)

        starts = jnp.arange(STRETCH_TOKENS // block, dtype=jnp.int32) * block
        outs = lax.map(one_block, starts)
        return outs.transpose(0, 2, 1, 3).reshape(STRETCH_TOKENS, query_group, HEAD_SIZE)

    stretch_out = lax.map(stretch_head, (current_query, keys, vals))
    stretch_out = stretch_out.transpose(1, 0, 2, 3).reshape(STRETCH_TOKENS, QUERY_HEADS * HEAD_SIZE).astype(jnp.bfloat16)

    suffix_query = suffix_queries.reshape(SUFFIX_SETS, SET_SLOTS, KEY_VALUE_HEADS, query_group, HEAD_SIZE)
    suffix_key_value = suffix_key_values.reshape(SUFFIX_SETS, SET_SLOTS, KEY_VALUE_HEADS, 2, HEAD_SIZE)
    slot_pos = jnp.arange(SET_SLOTS, dtype=jnp.int32)

    def single_set(operands):
        q_set, kv_set, length, starts = operands
        passage = jnp.sum((starts[None, :] <= slot_pos[:, None]).astype(jnp.int32), axis=1) - 1
        own_rows = (slot_pos[None, :] <= slot_pos[:, None]) & (passage[None, :] == passage[:, None]) & (slot_pos[None, :] < length)
        mask = jnp.concatenate([jnp.ones((SET_SLOTS, PREFIX_TOKENS + STRETCH_TOKENS), dtype=bool), own_rows], axis=1)

        def one_head(head_ops):
            q_head, k_head, v_head, own_k, own_v = head_ops
            return attend(q_head, jnp.concatenate([k_head, own_k], 0), jnp.concatenate([v_head, own_v], 0), mask)

        outs = lax.map(one_head, (q_set.transpose(1, 0, 2, 3), keys, vals,
                                  kv_set[:, :, 0].transpose(1, 0, 2), kv_set[:, :, 1].transpose(1, 0, 2)))
        outs = outs.transpose(2, 0, 1, 3).reshape(SET_SLOTS, QUERY_HEADS * HEAD_SIZE)
        return jnp.where((slot_pos < length)[:, None], outs, 0.0)

    suffix_output = lax.map(single_set, (suffix_query, suffix_key_value, set_length, passage_first_slot))
    suffix_output = suffix_output.reshape(SUFFIX_SLOTS, QUERY_HEADS * HEAD_SIZE).astype(jnp.bfloat16)
    return stretch_out, suffix_output
```

```python
import functools
import math

import jax
import jax.numpy as jnp
import numpy as np
from jax import lax
from jax.experimental import pallas as pl
from jax.experimental.pallas import tpu as pltpu
from jax.sharding import PartitionSpec as P

HEAD_SIZE = 128
GROUP = 8
PAIR = 2 * HEAD_SIZE
RATE = HEAD_SIZE ** (-0.5) * math.log2(math.e)
LOW = -1e30
VMEM_LIMIT = 40 * 1024 * 1024


def ring_order(count):
    wide = max(1, math.isqrt(count // 2))
    if count % wide or wide % 2 or wide < 2:
        return list(range(count))
    tall = count // wide
    order = [z * wide for z in range(tall)]
    for step, z in enumerate(reversed(range(tall))):
        row = [z * wide + x for x in range(1, wide)]
        order += row if step % 2 == 0 else row[::-1]
    return order


def split_columns(me, arrays, peers):
    rows = [a.shape[0] for a in arrays]
    cols = arrays[0].shape[1] // peers
    total = sum(rows)

    def kernel(me_ref, *refs):
        ins, outs = refs[: len(arrays)], refs[len(arrays) :]
        for r in range(peers):
            start = pl.multiple_of((me_ref[0] ^ r) * cols, HEAD_SIZE)
            top = 0
            for ref, count in zip(ins, rows):
                outs[r][top : top + count, :] = ref[:, pl.ds(start, cols)]
                top += count

    return pl.pallas_call(
        kernel,
        out_shape=[jax.ShapeDtypeStruct((total, cols), arrays[0].dtype)] * peers,
        in_specs=[pl.BlockSpec(memory_space=pltpu.SMEM)] + [pl.BlockSpec(memory_space=pltpu.VMEM)] * len(arrays),
        out_specs=[pl.BlockSpec(memory_space=pltpu.VMEM)] * peers,
        name="split_columns",
    )(me, *arrays)


def join_columns(me, chunks, rows):
    parts, peers = len(chunks), len(chunks[0])
    cols = chunks[0][0].shape[1]
    outs_count = chunks[0][0].shape[0] // rows
    flat = [c for part in chunks for c in part]

    def kernel(me_ref, *refs):
        ins, outs = refs[: len(flat)], refs[len(flat) :]
        for part in range(parts):
            for r in range(peers):
                start = pl.multiple_of((me_ref[0] ^ r) * (cols * parts) + part * cols, HEAD_SIZE)
                for o in range(outs_count):
                    outs[o][:, pl.ds(start, cols)] = ins[part * peers + r][o * rows : (o + 1) * rows, :]

    return pl.pallas_call(
        kernel,
        out_shape=[jax.ShapeDtypeStruct((rows, cols * parts * peers), flat[0].dtype)] * outs_count,
        in_specs=[pl.BlockSpec(memory_space=pltpu.SMEM)] + [pl.BlockSpec(memory_space=pltpu.VMEM)] * len(flat),
        out_specs=[pl.BlockSpec(memory_space=pltpu.VMEM)] * outs_count,
        name="join_columns",
    )(me, *flat)


def attend(info, queries, carry, prefixes, stretches, flags, own, last, split=4):
    peers = len(queries)
    tokens = queries[0].shape[0] // 2
    seat_tokens = peers * tokens
    heads = prefixes[0].shape[1] // PAIR
    groups = GROUP // split
    block = groups * seat_tokens
    pieces = list(prefixes) + list(stretches) + (list(own) if own else [])
    sizes = [p.shape[0] for p in pieces]
    keys = sum(sizes)
    n_prefix = sum(p.shape[0] for p in prefixes)
    n_common = n_prefix + sum(p.shape[0] for p in stretches)
    n_in = 1 + peers + len(pieces) + (2 if carry else 0)

    def kernel(*refs):
        info_ref = refs[0]
        q_refs = refs[1 : 1 + peers]
        piece_refs = refs[1 + peers : 1 + peers + len(pieces)]
        carry_refs = refs[1 + peers + len(pieces) : n_in]
        out_refs = refs[n_in:-2]
        k_ref, v_ref = refs[-2:]
        me = info_ref[0]

        @pl.when(pl.program_id(1) == 0)
        def _():
            top = 0
            for ref, size in zip(piece_refs, sizes):
                k_ref[top : top + size, :] = ref[:, :HEAD_SIZE]
                v_ref[top : top + size, :HEAD_SIZE] = ref[:, HEAD_SIZE:]
                top += size
            v_ref[:, HEAD_SIZE:] = jnp.ones((keys, HEAD_SIZE), jnp.bfloat16)

        def positions(axis):
            index = lax.broadcasted_iota(jnp.int32, (seat_tokens, seat_tokens), axis)
            return (me ^ (index // tokens)) * tokens + index % tokens

        row_pos = col_pos = None
        if own or last:
            row_pos = positions(0)
        if own:
            col_pos = positions(1)

        def scores(q, low, high):
            return lax.dot_general(
                q, k_ref[low:high, :], (((1,), (1,)), ((), ())), preferred_element_type=jnp.float32
            )

        for kind in range(2):
            q = jnp.concatenate(
                [
                    q_refs[r][kind * tokens : (kind + 1) * tokens, g * HEAD_SIZE : (g + 1) * HEAD_SIZE]
                    for g in range(groups)
                    for r in range(peers)
                ],
                axis=0,
            )
            spans = [(0, n_prefix, None)]
            top = n_prefix
            if kind == 0:
                for piece, flag in zip(stretches, flags):
                    spans.append((top, top + piece.shape[0], info_ref[flag] > 0))
                    top += piece.shape[0]
            else:
                spans = [(0, n_common + (seat_tokens if own else 0), None)]
            if own:
                if kind == 0:
                    allowed = col_pos <= row_pos
                    low, high = n_common, n_common + seat_tokens
                else:
                    row_set = col_set = jnp.zeros((seat_tokens, seat_tokens), jnp.int32)
                    for slot in range(4):
                        row_set += (info_ref[2 + slot] <= row_pos).astype(jnp.int32)
                        col_set += (info_ref[2 + slot] <= col_pos).astype(jnp.int32)
                    allowed = (col_pos <= row_pos) & (row_set == col_set) & (col_pos < info_ref[1])
                    low, high = n_common + seat_tokens, n_common + 2 * seat_tokens
                spans.append((low, high, allowed))
            parts = []
            for low, high, allowed in spans:
                if low == high:
                    continue
                s = scores(q, low, high)
                if allowed is not None:
                    if allowed.ndim == 2:
                        s = jnp.where(allowed[None], s.reshape(groups, seat_tokens, high - low), LOW)
                        s = s.reshape(block, high - low)
                    else:
                        s = jnp.where(allowed, s, LOW)
                parts.append((low, high, s))
            peak = functools.reduce(jnp.maximum, [jnp.max(s, axis=1, keepdims=True) for _, _, s in parts])
            if carry:
                stats = carry_refs[1][0, kind]
                old = stats[:, :1]
                peak = jnp.maximum(old, peak)
                fade = jnp.exp2((old - peak) * RATE)
                acc = carry_refs[0][0, kind] * fade
                total = stats[:, HEAD_SIZE // 2 : HEAD_SIZE // 2 + 1] * fade
            else:
                acc = total = None
            for low, high, s in parts:
                weights = jnp.exp2((s - peak) * RATE).astype(jnp.bfloat16)
                both = jnp.dot(weights, v_ref[low:high, :], preferred_element_type=jnp.float32)
                if acc is None:
                    acc, total = both[:, :HEAD_SIZE], both[:, HEAD_SIZE:]
                else:
                    acc = acc + both[:, :HEAD_SIZE]
                    total = total + both[:, HEAD_SIZE:]
            if last:
                result = acc / total
                if kind == 1:
                    live = (row_pos < info_ref[1])[:, :HEAD_SIZE]
                    result = jnp.where(
                        live[None], result.reshape(groups, seat_tokens, HEAD_SIZE), 0.0
                    ).reshape(block, HEAD_SIZE)
                result = result.astype(jnp.bfloat16)
                for g in range(groups):
                    for r in range(peers):
                        row = g * seat_tokens + r * tokens
                        out_refs[r][kind * tokens : (kind + 1) * tokens, g * HEAD_SIZE : (g + 1) * HEAD_SIZE] = (
                            result[row : row + tokens]
                        )
            else:
                out_refs[0][0, kind] = acc
                lane = lax.broadcasted_iota(jnp.int32, (block, HEAD_SIZE), 1)
                out_refs[1][0, kind] = jnp.where(lane < HEAD_SIZE // 2, peak, total)

    state_spec = pl.BlockSpec((1, 2, block, HEAD_SIZE), lambda h, b: (h, 0, b, 0))
    state_shape = jax.ShapeDtypeStruct((heads, 2, GROUP * seat_tokens, HEAD_SIZE), jnp.float32)
    q_spec = pl.BlockSpec((2 * tokens, groups * HEAD_SIZE), lambda h, b: (0, h * split + b))
    in_specs = (
        [pl.BlockSpec(memory_space=pltpu.SMEM)]
        + [q_spec] * peers
        + [pl.BlockSpec((size, PAIR), lambda h, b: (0, h)) for size in sizes]
        + ([state_spec] * 2 if carry else [])
    )
    if last:
        out_shape = [jax.ShapeDtypeStruct(q.shape, jnp.bfloat16) for q in queries]
        out_specs = [q_spec] * peers
    else:
        out_shape = [state_shape] * 2
        out_specs = [state_spec] * 2
    rows = heads * GROUP * seat_tokens * 2
    return pl.pallas_call(
        kernel,
        grid=(heads, split),
        in_specs=in_specs,
        out_specs=out_specs,
        out_shape=out_shape,
        scratch_shapes=[
            pltpu.VMEM((keys, HEAD_SIZE), jnp.bfloat16),
            pltpu.VMEM((keys, PAIR), jnp.bfloat16),
        ],
        compiler_params=pltpu.CompilerParams(vmem_limit_bytes=VMEM_LIMIT),
        cost_estimate=pl.CostEstimate(
            flops=rows * keys * HEAD_SIZE * 8, bytes_accessed=rows * HEAD_SIZE * 8, transcendentals=rows * keys
        ),
        name="attend",
    )(info, *queries, *pieces, *(carry if carry else ()))


def body(
    stretch_queries,
    stretch_key_values,
    suffix_queries,
    suffix_key_values,
    prefix_key_values,
    set_length,
    passage_first_slot,
    *,
    peers,
    seats,
):
    tokens = stretch_queries.shape[0]
    me = lax.axis_index("head").astype(jnp.int32)
    seat = lax.axis_index("seq").astype(jnp.int32)
    order = ring_order(seats)
    place = {s: i for i, s in enumerate(order)}
    right = [(order[i], order[(i + 1) % seats]) for i in range(seats)]
    left = [(b, a) for a, b in right]
    across = [[(h, h ^ r) for h in range(peers)] for r in range(peers)]
    half = seats // 2

    table = np.zeros((seats, 2 * half), np.int32)
    for s in range(seats):
        for k in range(1, half + 1):
            table[s, 2 * k - 2] = order[(place[s] - k) % seats] < s
            table[s, 2 * k - 1] = order[(place[s] + k) % seats] < s
    sees = lax.dynamic_slice_in_dim(jnp.asarray(table), seat, 1, 0)[0]
    me = me[None]
    info = jnp.concatenate([me, set_length, passage_first_slot[0], sees])
    first_flag = 2 + passage_first_slot.shape[1]

    def around(first):
        from_left, from_right = first, first
        arrived = []
        for step in range(1, half + 1):
            if step == half:
                cut = first.shape[0] // 2
                from_left, from_right = from_left[:cut], from_right[cut:]
            from_left = lax.ppermute(from_left, "seq", right)
            from_right = lax.ppermute(from_right, "seq", left)
            arrived.append((from_left, from_right))
        return arrived

    key_value_chunks = split_columns(me, [stretch_key_values, suffix_key_values], peers)
    key_value_chunks = [key_value_chunks[0]] + [
        lax.ppermute(key_value_chunks[r], "head", across[r]) for r in range(1, peers)
    ]
    queries = split_columns(me, [stretch_queries, suffix_queries], peers)
    queries = [queries[0]] + [lax.ppermute(queries[r], "head", across[r]) for r in range(1, peers)]
    own_stretch = jnp.concatenate([c[:tokens] for c in key_value_chunks], axis=0)
    own_suffix = jnp.concatenate([c[tokens:] for c in key_value_chunks], axis=0)

    prefix = around(prefix_key_values)
    stretch = around(own_stretch)

    def update(carry, first, stop, own, last):
        prefixes = [p for k in range(first, stop) for p in prefix[k]]
        stretches = [p for k in range(first, stop) for p in stretch[k]]
        flags = [first_flag + 2 * k + side for k in range(first, stop) for side in range(2)]
        if own:
            prefixes = [prefix_key_values] + prefixes
        return attend(info, queries, carry, prefixes, stretches, flags, own, last)

    early = max(1, half - 2)
    carry = update(None, 0, early, (own_stretch, own_suffix), False)
    if half - 1 > early:
        carry = update(carry, early, half - 1, None, False)
    outs = update(carry, half - 1, half, None, True)
    outs = [outs[0]] + [lax.ppermute(outs[r], "head", across[r]) for r in range(1, peers)]
    return tuple(join_columns(me, [outs], tokens))


def solution(mesh):
    placed = (
        P(("seq", "head"), None),
        P(("seq", "head"), None),
        P(("seq", "head"), None),
        P(("seq", "head"), None),
        P("seq", "head"),
        P("seq"),
        P("seq", None),
    )
    return jax.shard_map(
        functools.partial(body, peers=mesh.shape["head"], seats=mesh.shape["seq"]),
        mesh=mesh,
        in_specs=placed,
        out_specs=(P(("seq", "head"), None), P(("seq", "head"), None)),
        check_vma=False,
    )
```

```python
import functools
import math

import jax
import jax.numpy as jnp
import numpy as np
from jax import lax
from jax.experimental import pallas as pl
from jax.experimental.pallas import tpu as pltpu
from jax.sharding import PartitionSpec as P

HEAD_SIZE = 128
GROUP = 8
PAIR = 2 * HEAD_SIZE
RATE = HEAD_SIZE ** (-0.5) * math.log2(math.e)
LOW = -1e30
PASSAGES = 4
MERGE = 2
TIE_P = True
TIE_Q = True
VMEM_LIMIT = 40 * 1024 * 1024


def ring_order(count):
    wide = max(1, math.isqrt(count // 2))
    if count % wide or wide % 2 or wide < 2:
        return list(range(count))
    tall = count // wide
    order = [z * wide for z in range(tall)]
    for step, z in enumerate(reversed(range(tall))):
        row = [z * wide + x for x in range(1, wide)]
        order += row if step % 2 == 0 else row[::-1]
    return order


def is_one_of(index, members):
    found = jnp.int32(0)
    for base in range(0, max(members, default=0) + 1, 16):
        bits = sum(1 << (m - base) for m in members if base <= m < base + 16)
        found += jnp.where(index // 16 == base // 16, (jnp.int32(bits) >> (index % 16)) & 1, 0)
    return found > 0


def split_columns(arrays, peers):
    rows = [a.shape[0] for a in arrays]
    cols = arrays[0].shape[1] // peers
    total = sum(rows)

    def kernel(*refs):
        ins, outs = refs[: len(arrays)], refs[len(arrays) :]
        me = lax.axis_index("head")
        for r in range(peers):
            start = pl.multiple_of((me ^ r) * cols, HEAD_SIZE)
            top = 0
            for ref, count in zip(ins, rows):
                outs[r][top : top + count, :] = ref[:, pl.ds(start, cols)]
                top += count

    return pl.pallas_call(
        kernel,
        out_shape=[jax.ShapeDtypeStruct((total, cols), arrays[0].dtype)] * peers,
        in_specs=[pl.BlockSpec(memory_space=pltpu.VMEM)] * len(arrays),
        out_specs=[pl.BlockSpec(memory_space=pltpu.VMEM)] * peers,
        name="split_columns",
    )(*arrays)


def join_columns(chunks, rows):
    parts, peers = len(chunks), len(chunks[0])
    cols = chunks[0][0].shape[1]
    outs_count = chunks[0][0].shape[0] // rows
    flat = [c for part in chunks for c in part]

    def kernel(*refs):
        ins, outs = refs[: len(flat)], refs[len(flat) :]
        me = lax.axis_index("head")
        for part in range(parts):
            for r in range(peers):
                start = pl.multiple_of((me ^ r) * (cols * parts) + part * cols, HEAD_SIZE)
                for o in range(outs_count):
                    outs[o][:, pl.ds(start, cols)] = ins[part * peers + r][o * rows : (o + 1) * rows, :]

    return pl.pallas_call(
        kernel,
        out_shape=[jax.ShapeDtypeStruct((rows, cols * parts * peers), flat[0].dtype)] * outs_count,
        in_specs=[pl.BlockSpec(memory_space=pltpu.VMEM)] * len(flat),
        out_specs=[pl.BlockSpec(memory_space=pltpu.VMEM)] * outs_count,
        name="join_columns",
    )(*flat)


def stack_rows(groups):
    flat = []
    for group in groups:
        for array, _, _ in group:
            if not any(array is other for other in flat):
                flat.append(array)

    def kernel(*refs):
        ins, outs = refs[: len(flat)], refs[len(flat) :]
        for group, out in zip(groups, outs):
            top = 0
            for array, low, count in group:
                source = [ref for ref, other in zip(ins, flat) if other is array][0]
                out[top : top + count, :] = source[low : low + count, :]
                top += count

    return pl.pallas_call(
        kernel,
        out_shape=[
            jax.ShapeDtypeStruct((sum(count for _, _, count in group), group[0][0].shape[1]), group[0][0].dtype)
            for group in groups
        ],
        in_specs=[pl.BlockSpec(memory_space=pltpu.VMEM)] * len(flat),
        out_specs=[pl.BlockSpec(memory_space=pltpu.VMEM)] * len(groups),
        name="stack_rows",
    )(*flat)


def attend(length, starts, peers, sets, pieces, own, last):
    first = [state is None for _, _, state in sets]
    tokens = sets[0][1][0].shape[0] // 2 if first[0] else sets[0][1].shape[3] // (len(sets[0][0]) * GROUP)
    seat_tokens = peers * tokens
    heads = pieces[0][0].shape[1] // PAIR
    arrays = [p[0] for p in pieces] + list(own or ())
    prefix_rows = [p[1] for p in pieces]
    stretch_rows = [p[0].shape[0] - p[1] for p in pieces]
    seen_by = [p[2] for p in pieces]
    n_prefix = sum(prefix_rows)
    n_common = n_prefix + sum(stretch_rows)
    keys = n_common + (2 * seat_tokens if own else 0)

    flat = [length, starts] + arrays
    q_at, state_at = [], []
    for (ranks, queries, state), fresh in zip(sets, first):
        q_at.append(len(flat))
        flat += list(queries) if fresh else [queries]
        state_at.append(len(flat))
        flat += [] if fresh else list(state)

    mine = [len(ranks) * tokens for ranks, _, _ in sets]
    blocks = [GROUP * m for m in mine]
    out_shape, out_at = [], []
    for (ranks, _, _), fresh, block in zip(sets, first, blocks):
        out_at.append(len(out_shape))
        if last:
            out_shape += [jax.ShapeDtypeStruct((2 * tokens, heads * GROUP * HEAD_SIZE), jnp.bfloat16)] * len(ranks)
        else:
            out_shape.append(jax.ShapeDtypeStruct((heads, 2, HEAD_SIZE, block), jnp.float32))
            out_shape.append(jax.ShapeDtypeStruct((heads, 2, 8, block), jnp.float32))
            if fresh:
                out_shape.append(jax.ShapeDtypeStruct((heads, 2, HEAD_SIZE, block), jnp.bfloat16))

    def kernel(*refs):
        length_ref, starts_ref, array_refs = refs[0], refs[1], refs[2 : 2 + len(arrays)]
        in_refs, out_refs = refs[: len(flat)], refs[len(flat) : -2]
        k_ref, v_ref = refs[-2:]
        me = lax.axis_index("head")
        seat = lax.axis_index("seq")

        def query_positions(n, rows):
            index = lax.broadcasted_iota(jnp.int32, (rows, mine[n]), 1)
            rank = jnp.full_like(index, sets[n][0][0])
            for i, r in enumerate(sets[n][0][1:]):
                rank = jnp.where(index // tokens == i + 1, r, rank)
            return (me ^ rank) * tokens + index % tokens

        def tiled(allowed):
            return jnp.concatenate([jnp.where(allowed, 0.0, LOW)] * GROUP, axis=1)

        masks, live = [], []
        for n in range(len(sets)):
            if own:
                q_pos = query_positions(n, seat_tokens)
                index = lax.broadcasted_iota(jnp.int32, (seat_tokens, mine[n]), 0)
                k_pos = (me ^ (index // tokens)) * tokens + index % tokens
                before = k_pos <= q_pos
                q_set = k_set = jnp.zeros((seat_tokens, mine[n]), jnp.int32)
                for slot in range(PASSAGES):
                    q_set += (starts_ref[0, slot] <= q_pos).astype(jnp.int32)
                    k_set += (starts_ref[0, slot] <= k_pos).astype(jnp.int32)
                masks.append((tiled(before), tiled(before & (q_set == k_set) & (k_pos < length_ref[0]))))
            if last:
                live.append(tiled(query_positions(n, 1) < length_ref[0]) == 0.0)

        def load(h):
            base = h * PAIR

            def put(ref, low, count, top):
                k_ref[h, top : top + count, :] = ref[low : low + count, base : base + HEAD_SIZE]
                v_ref[h, :HEAD_SIZE, top : top + count] = jnp.transpose(
                    ref[low : low + count, base + HEAD_SIZE : base + PAIR]
                )

            top, low = 0, n_prefix
            for ref, in_prefix, in_stretch in zip(array_refs, prefix_rows, stretch_rows):
                if in_prefix:
                    put(ref, 0, in_prefix, top)
                if in_stretch:
                    put(ref, in_prefix, in_stretch, low)
                top += in_prefix
                low += in_stretch
            for ref in array_refs[len(pieces) :]:
                put(ref, 0, seat_tokens, low)
                low += seat_tokens
            v_ref[h, HEAD_SIZE:, :] = jnp.ones((16, keys), jnp.bfloat16)

        def look(n, h, kind):
            if first[n]:
                q = jnp.concatenate(
                    [
                        ref[kind * tokens : (kind + 1) * tokens, col * HEAD_SIZE : (col + 1) * HEAD_SIZE]
                        for col in range(h * GROUP, (h + 1) * GROUP)
                        for ref in in_refs[q_at[n] : state_at[n]]
                    ],
                    axis=0,
                )
                q = jnp.transpose(q)
                if not last:
                    out_refs[out_at[n] + 2][h, kind] = q
            else:
                q = in_refs[q_at[n]][h, kind]
            if kind == 0:
                spans = [(0, n_prefix, None)]
                top = n_prefix
                for count, seen in zip(stretch_rows, seen_by):
                    if count:
                        spans.append((top, top + count, is_one_of(seat, seen)))
                    top += count
                if own:
                    spans.append((n_common, n_common + seat_tokens, masks[n][0]))
            else:
                spans = [(0, n_common + (seat_tokens if own else 0), None)]
                if own:
                    spans.append((n_common + seat_tokens, n_common + 2 * seat_tokens, masks[n][1]))
            parts = []
            for low, high, allowed in spans:
                if low == high:
                    continue
                s = jnp.dot(k_ref[h, low:high, :], q, preferred_element_type=jnp.float32)
                if allowed is not None:
                    s = s + allowed if allowed.ndim == 2 else jnp.where(allowed, s, LOW)
                parts.append(s)
            return parts, functools.reduce(jnp.maximum, [jnp.max(s, axis=0, keepdims=True) for s in parts])

        def weigh(n, h, kind, parts, peak):
            if not first[n]:
                acc_ref, stats_ref = in_refs[state_at[n]], in_refs[state_at[n] + 1]
                old = stats_ref[h, kind, 0:1, :]
                peak = jnp.maximum(old, peak)
                fade = jnp.exp2((old - peak) * RATE)
            weights = jnp.concatenate([jnp.exp2((s - peak) * RATE).astype(jnp.bfloat16) for s in parts], axis=0)
            both = jnp.dot(v_ref[h, :, : weights.shape[0]], weights, preferred_element_type=jnp.float32)
            acc, total = both[:HEAD_SIZE], both[HEAD_SIZE : HEAD_SIZE + 1]
            if not first[n]:
                acc = acc + acc_ref[h, kind] * fade
                total = total + stats_ref[h, kind, 1:2, :] * fade
            if not last:
                out_refs[out_at[n]][h, kind] = acc
                out_refs[out_at[n] + 1][h, kind, 0:1, :] = peak
                out_refs[out_at[n] + 1][h, kind, 1:2, :] = total
                return
            result = acc * (1.0 / total)
            if kind == 1:
                result = jnp.where(live[n], result, 0.0)
            result = jnp.transpose(result.astype(jnp.bfloat16))
            for g in range(GROUP):
                col = (h * GROUP + g) * HEAD_SIZE
                for i in range(len(sets[n][0])):
                    row = g * mine[n] + i * tokens
                    out_refs[out_at[n] + i][kind * tokens : (kind + 1) * tokens, col : col + HEAD_SIZE] = result[
                        row : row + tokens
                    ]

        items = [(n, h, kind) for h in range(heads) for n in range(len(sets)) for kind in range(2)]
        for h in range(heads):
            load(h)
        ahead = look(*items[0])
        for i, item in enumerate(items):
            now = ahead
            if i + 1 < len(items):
                ahead = look(*items[i + 1])
            weigh(*item, *now)

    vmem = pl.BlockSpec(memory_space=pltpu.VMEM)
    rows = heads * 2 * sum(blocks)
    outs = pl.pallas_call(
        kernel,
        in_specs=[pl.BlockSpec(memory_space=pltpu.SMEM)] * 2 + [vmem] * (len(flat) - 2),
        out_specs=[vmem] * len(out_shape),
        out_shape=out_shape,
        scratch_shapes=[
            pltpu.VMEM((heads, keys, HEAD_SIZE), jnp.bfloat16),
            pltpu.VMEM((heads, HEAD_SIZE + 16, keys), jnp.bfloat16),
        ],
        compiler_params=pltpu.CompilerParams(vmem_limit_bytes=VMEM_LIMIT),
        cost_estimate=pl.CostEstimate(
            flops=rows * keys * HEAD_SIZE * 8, bytes_accessed=rows * HEAD_SIZE * 8, transcendentals=rows * keys
        ),
        name="attend",
    )(*flat)
    after = []
    for n, (ranks, queries, _) in enumerate(sets):
        got = outs[out_at[n] :]
        if last:
            after.append(got[: len(ranks)])
        else:
            after.append((ranks, got[2] if first[n] else queries, (got[0], got[1])))
    return after


def body(
    stretch_queries,
    stretch_key_values,
    suffix_queries,
    suffix_key_values,
    prefix_key_values,
    set_length,
    passage_first_slot,
    *,
    peers,
    seats,
):
    tokens = stretch_queries.shape[0]
    prefix_tokens = prefix_key_values.shape[0]
    seat_tokens = peers * tokens
    me = lax.axis_index("head").astype(jnp.int32)
    seat = lax.axis_index("seq").astype(jnp.int32)
    order = ring_order(seats)
    place = {s: i for i, s in enumerate(order)}
    right = [(order[i], order[(i + 1) % seats]) for i in range(seats)]
    left = [(b, a) for a, b in right]
    half = seats // 2

    def across(chunk, r):
        return lax.ppermute(chunk, "head", [(h, h ^ r) for h in range(peers)])

    def step(from_left, from_right):
        return lax.ppermute(from_left, "seq", right), lax.ppermute(from_right, "seq", left)

    def seers(k, side):
        return [s for s in range(seats) if order[(place[s] + (k if side else -k)) % seats] < s]

    near = tuple(r for r in range(peers) if r < 2)
    far = tuple(r for r in range(peers) if r >= 2)

    prefix = {1: step(prefix_key_values, prefix_key_values)}
    chunks = split_columns([stretch_key_values, suffix_key_values], peers)
    chunks = [chunks[0]] + [across(chunks[r], r) for r in range(1, peers)]
    queries = split_columns([stretch_queries, suffix_queries], peers)
    own = stack_rows([[(c, 0, tokens) for c in chunks], [(c, tokens, tokens) for c in chunks]])
    own_stretch = own[0]
    if TIE_P:
        own_stretch, prefix[1] = lax.optimization_barrier((own_stretch, prefix[1]))
    if TIE_Q:
        own_stretch, queries = lax.optimization_barrier((own_stretch, queries))
    queries = [queries[0]] + [across(queries[r], r) for r in range(1, peers)]
    stretch = {1: step(own_stretch, own_stretch)}

    pieces = {0: [(prefix_key_values, prefix_tokens, [])]}
    for k in range(1, min(MERGE, half + 1)):
        if k > 1:
            pair = [prefix[k - 1], stretch[k - 1]]
            if k == half:
                pair = [(p[0][: p[0].shape[0] // 2], p[1][p[1].shape[0] // 2 :]) for p in pair]
            prefix[k] = step(*pair[0])
            stretch[k] = step(*pair[1])
        pieces[k] = [(p, p.shape[0], []) for p in prefix[k]]
        pieces[k] += [(s, 0, seers(k, side)) for side, s in enumerate(stretch[k])]
    k = MERGE - 1
    if k < half:
        whole = stack_rows(
            [[(prefix[k][side], 0, prefix_tokens), (stretch[k][side], 0, seat_tokens)] for side in range(2)]
        )
    for k in range(MERGE, half + 1):
        counts = [prefix_tokens, prefix_tokens]
        if k == half:
            cut = (prefix_tokens + seat_tokens) // 2
            whole = whole[0][:cut], whole[1][cut:]
            counts = [min(cut, prefix_tokens), max(0, prefix_tokens - cut)]
        whole = step(*whole)
        pieces[k] = [(whole[side], counts[side], seers(k, side)) for side in range(2)]

    near_set, far_set = (near, [queries[r] for r in near], None), (far, [queries[r] for r in far], None)
    (near_set,) = attend(set_length, passage_first_slot, peers, [near_set], pieces[0], own, False)
    (near_set,) = attend(set_length, passage_first_slot, peers, [near_set], pieces[1], None, False)
    (far_set,) = attend(set_length, passage_first_slot, peers, [far_set], pieces[0] + pieces[1], own, False)
    for k in range(2, half):
        near_set, far_set = attend(set_length, passage_first_slot, peers, [near_set, far_set], pieces[k], None, False)
    (far_out,) = attend(set_length, passage_first_slot, peers, [far_set], pieces[half], None, True)
    (near_out,) = attend(set_length, passage_first_slot, peers, [near_set], pieces[half], None, True)
    outs = list(near_out) + list(far_out)
    outs = [outs[0]] + [across(outs[r], r) for r in range(1, peers)]
    return tuple(join_columns([outs], tokens))


def solution(mesh):
    placed = (
        P(("seq", "head"), None),
        P(("seq", "head"), None),
        P(("seq", "head"), None),
        P(("seq", "head"), None),
        P("seq", "head"),
        P("seq"),
        P("seq", None),
    )
    return jax.shard_map(
        functools.partial(body, peers=mesh.shape["head"], seats=mesh.shape["seq"]),
        mesh=mesh,
        in_specs=placed,
        out_specs=(P(("seq", "head"), None), P(("seq", "head"), None)),
        check_vma=False,
    )
```

```python
import functools
import math

import jax
import jax.numpy as jnp
import numpy as np
from jax import lax
from jax.experimental import pallas as pl
from jax.experimental.pallas import tpu as pltpu
from jax.sharding import PartitionSpec as P

HEAD_SIZE = 128
GROUP = 8
PAIR = 2 * HEAD_SIZE
RATE = HEAD_SIZE ** (-0.5) * math.log2(math.e)
LOW = -1e30
PASSAGES = 4
AHEAD = 3
JOIN_VMEM = 8 * 1024 * 1024
VMEM_LIMIT = 40 * 1024 * 1024


def ring_order(count):
    wide = max(1, math.isqrt(count // 2))
    if count % wide or wide % 2 or wide < 2:
        return list(range(count))
    tall = count // wide
    order = [z * wide for z in range(tall)]
    for step, z in enumerate(reversed(range(tall))):
        row = [z * wide + x for x in range(1, wide)]
        order += row if step % 2 == 0 else row[::-1]
    return order


def is_one_of(index, members):
    found = jnp.int32(0)
    for base in range(0, max(members, default=0) + 1, 16):
        bits = sum(1 << (m - base) for m in members if base <= m < base + 16)
        found += jnp.where(index // 16 == base // 16, (jnp.int32(bits) >> (index % 16)) & 1, 0)
    return found > 0


def split_columns(arrays, peers):
    cols = arrays[0].shape[1] // peers
    me = lax.axis_index("head")
    return [
        jnp.concatenate([lax.dynamic_slice_in_dim(a, (me ^ r) * cols, cols, 1) for a in arrays], axis=0)
        for r in range(peers)
    ]


def join_columns(chunks, peers, rows):
    cols = chunks[0].shape[1]
    count = chunks[0].shape[0] // rows

    def kernel(*refs):
        ins, outs = refs[:peers], refs[peers : peers + count]
        me = lax.axis_index("head")
        copies = []
        for r in range(peers):
            start = pl.multiple_of((me ^ r) * cols, HEAD_SIZE)
            for o in range(count):
                source, target = ins[r].at[pl.ds(o * rows, rows)], outs[o].at[:, pl.ds(start, cols)]
                copies.append(pltpu.make_async_copy(source, target, refs[-1].at[r, o]))
        for copy in copies:
            copy.start()
        for copy in copies:
            copy.wait()

    return pl.pallas_call(
        kernel,
        out_shape=[jax.ShapeDtypeStruct((rows, cols * peers), chunks[0].dtype)] * count,
        in_specs=[pl.BlockSpec(memory_space=pltpu.VMEM)] * peers,
        out_specs=[pl.BlockSpec(memory_space=pl.ANY)] * count,
        scratch_shapes=[pltpu.SemaphoreType.DMA((peers, count))],
        compiler_params=pltpu.CompilerParams(vmem_limit_bytes=JOIN_VMEM),
        name="join_columns",
    )(*chunks)


def attend(length, starts, peers, sets, pieces, own, last):
    first = [state is None for _, _, state in sets]
    tokens = sets[0][1][0].shape[0] // 2 if first[0] else sets[0][1].shape[3] // (len(sets[0][0]) * GROUP)
    seat_tokens = peers * tokens
    heads = pieces[0][0].shape[1] // PAIR
    arrays = [p[0] for p in pieces] + list(own or ())
    spots = [(i,) + span for i, (_, spans) in enumerate(pieces) for span in spans]
    spots = [s for s in spots if s[3] is None] + [s for s in spots if s[3] is not None]
    n_prefix = sum(s[2] for s in spots if s[3] is None)
    n_common = sum(s[2] for s in spots)
    keys = n_common + (2 * seat_tokens if own else 0)

    flat = [length, starts] + arrays
    q_at, state_at = [], []
    for (ranks, queries, state), fresh in zip(sets, first):
        q_at.append(len(flat))
        flat += list(queries) if fresh else [queries]
        state_at.append(len(flat))
        flat += [] if fresh else list(state)

    mine = [len(ranks) * tokens for ranks, _, _ in sets]
    blocks = [GROUP * m for m in mine]
    out_shape, out_at = [], []
    for (ranks, _, _), fresh, block in zip(sets, first, blocks):
        out_at.append(len(out_shape))
        if last:
            out_shape += [jax.ShapeDtypeStruct((2 * tokens, heads * GROUP * HEAD_SIZE), jnp.bfloat16)] * len(ranks)
        else:
            out_shape.append(jax.ShapeDtypeStruct((heads, 2, HEAD_SIZE, block), jnp.float32))
            out_shape.append(jax.ShapeDtypeStruct((heads, 2, 8, block), jnp.float32))
            if fresh:
                out_shape.append(jax.ShapeDtypeStruct((heads, 2, HEAD_SIZE, block), jnp.bfloat16))

    def kernel(*refs):
        length_ref, starts_ref, array_refs = refs[0], refs[1], refs[2 : 2 + len(arrays)]
        in_refs, out_refs = refs[: len(flat)], refs[len(flat) : -2]
        k_ref, v_ref = refs[-2:]
        me = lax.axis_index("head")
        seat = lax.axis_index("seq")

        def query_positions(n, rows):
            index = lax.broadcasted_iota(jnp.int32, (rows, mine[n]), 1)
            rank = jnp.full_like(index, sets[n][0][0])
            for i, r in enumerate(sets[n][0][1:]):
                rank = jnp.where(index // tokens == i + 1, r, rank)
            return (me ^ rank) * tokens + index % tokens

        def tiled(allowed):
            return jnp.concatenate([jnp.where(allowed, 0.0, LOW)] * GROUP, axis=1)

        masks, live = [], []
        for n in range(len(sets)):
            if own:
                q_pos = query_positions(n, seat_tokens)
                index = lax.broadcasted_iota(jnp.int32, (seat_tokens, mine[n]), 0)
                k_pos = (me ^ (index // tokens)) * tokens + index % tokens
                before = k_pos <= q_pos
                q_set = k_set = jnp.zeros((seat_tokens, mine[n]), jnp.int32)
                for slot in range(PASSAGES):
                    q_set += (starts_ref[0, slot] <= q_pos).astype(jnp.int32)
                    k_set += (starts_ref[0, slot] <= k_pos).astype(jnp.int32)
                masks.append((tiled(before), tiled(before & (q_set == k_set) & (k_pos < length_ref[0]))))
            if last:
                live.append(tiled(query_positions(n, 1) < length_ref[0]) == 0.0)

        def load(h):
            base = h * PAIR

            def put(ref, low, count, top):
                k_ref[h, top : top + count, :] = ref[low : low + count, base : base + HEAD_SIZE]
                v_ref[h, :HEAD_SIZE, top : top + count] = jnp.transpose(
                    ref[low : low + count, base + HEAD_SIZE : base + PAIR]
                )

            top = 0
            for i, low, count, _ in spots:
                put(array_refs[i], low, count, top)
                top += count
            for ref in array_refs[len(pieces) :]:
                put(ref, 0, seat_tokens, top)
                top += seat_tokens
            v_ref[h, HEAD_SIZE:, :] = jnp.ones((16, keys), jnp.bfloat16)

        def look(n, h, kind):
            if first[n]:
                q = jnp.concatenate(
                    [
                        ref[kind * tokens : (kind + 1) * tokens, col * HEAD_SIZE : (col + 1) * HEAD_SIZE]
                        for col in range(h * GROUP, (h + 1) * GROUP)
                        for ref in in_refs[q_at[n] : state_at[n]]
                    ],
                    axis=0,
                )
                q = jnp.transpose(q)
                if not last:
                    out_refs[out_at[n] + 2][h, kind] = q
            else:
                q = in_refs[q_at[n]][h, kind]
            if kind == 0:
                spans = [(0, n_prefix, None)]
                top = n_prefix
                for _, _, count, seen in spots:
                    if seen is not None:
                        spans.append((top, top + count, is_one_of(seat, seen)))
                        top += count
                if own:
                    spans.append((n_common, n_common + seat_tokens, masks[n][0]))
            else:
                spans = [(0, n_common + (seat_tokens if own else 0), None)]
                if own:
                    spans.append((n_common + seat_tokens, n_common + 2 * seat_tokens, masks[n][1]))
            parts = []
            for low, high, allowed in spans:
                if low == high:
                    continue
                s = jnp.dot(k_ref[h, low:high, :], q, preferred_element_type=jnp.float32)
                if allowed is not None:
                    s = s + allowed if allowed.ndim == 2 else jnp.where(allowed, s, LOW)
                parts.append(s)
            return parts, functools.reduce(jnp.maximum, [jnp.max(s, axis=0, keepdims=True) for s in parts])

        def weigh(n, h, kind, parts, peak):
            if not first[n]:
                acc_ref, stats_ref = in_refs[state_at[n]], in_refs[state_at[n] + 1]
                old = stats_ref[h, kind, 0:1, :]
                peak = jnp.maximum(old, peak)
                fade = jnp.exp2((old - peak) * RATE)
            weights = jnp.concatenate([jnp.exp2((s - peak) * RATE).astype(jnp.bfloat16) for s in parts], axis=0)
            both = jnp.dot(v_ref[h, :, : weights.shape[0]], weights, preferred_element_type=jnp.float32)
            acc, total = both[:HEAD_SIZE], both[HEAD_SIZE : HEAD_SIZE + 1]
            if not first[n]:
                acc = acc + acc_ref[h, kind] * fade
                total = total + stats_ref[h, kind, 1:2, :] * fade
            if not last:
                out_refs[out_at[n]][h, kind] = acc
                out_refs[out_at[n] + 1][h, kind, 0:1, :] = peak
                out_refs[out_at[n] + 1][h, kind, 1:2, :] = total
                return
            result = acc * (1.0 / total)
            if kind == 1:
                result = jnp.where(live[n], result, 0.0)
            result = jnp.transpose(result.astype(jnp.bfloat16))
            for g in range(GROUP):
                col = (h * GROUP + g) * HEAD_SIZE
                for i in range(len(sets[n][0])):
                    row = g * mine[n] + i * tokens
                    out_refs[out_at[n] + i][kind * tokens : (kind + 1) * tokens, col : col + HEAD_SIZE] = result[
                        row : row + tokens
                    ]

        items = [(n, h, kind) for h in range(heads) for n in range(len(sets)) for kind in range(2)]
        for h in range(heads):
            load(h)
        queue = [look(*item) for item in items[:AHEAD]]
        for i, item in enumerate(items):
            if i + AHEAD < len(items):
                queue.append(look(*items[i + AHEAD]))
            weigh(*item, *queue[i])

    vmem = pl.BlockSpec(memory_space=pltpu.VMEM)
    rows = heads * 2 * sum(blocks)
    outs = pl.pallas_call(
        kernel,
        in_specs=[pl.BlockSpec(memory_space=pltpu.SMEM)] * 2 + [vmem] * (len(flat) - 2),
        out_specs=[vmem] * len(out_shape),
        out_shape=out_shape,
        scratch_shapes=[
            pltpu.VMEM((heads, keys, HEAD_SIZE), jnp.bfloat16),
            pltpu.VMEM((heads, HEAD_SIZE + 16, keys), jnp.bfloat16),
        ],
        compiler_params=pltpu.CompilerParams(vmem_limit_bytes=VMEM_LIMIT),
        cost_estimate=pl.CostEstimate(
            flops=rows * keys * HEAD_SIZE * 8, bytes_accessed=rows * HEAD_SIZE * 8, transcendentals=rows * keys
        ),
        name="attend",
    )(*flat)
    after = []
    for n, (ranks, queries, _) in enumerate(sets):
        got = outs[out_at[n] :]
        if last:
            after.append(got[: len(ranks)])
        else:
            after.append((ranks, got[2] if first[n] else queries, (got[0], got[1])))
    return after


def body(
    stretch_queries,
    stretch_key_values,
    suffix_queries,
    suffix_key_values,
    prefix_key_values,
    set_length,
    passage_first_slot,
    *,
    peers,
    seats,
):
    tokens = stretch_queries.shape[0]
    prefix_tokens = prefix_key_values.shape[0]
    seat_tokens = peers * tokens
    me = lax.axis_index("head").astype(jnp.int32)
    seat = lax.axis_index("seq").astype(jnp.int32)
    order = ring_order(seats)
    place = {s: i for i, s in enumerate(order)}
    right = [(order[i], order[(i + 1) % seats]) for i in range(seats)]
    left = [(b, a) for a, b in right]
    half = seats // 2

    def across(chunk, r):
        return lax.ppermute(chunk, "head", [(h, h ^ r) for h in range(peers)])

    def step(from_left, from_right):
        return lax.ppermute(from_left, "seq", right), lax.ppermute(from_right, "seq", left)

    def seers(k, side):
        return [s for s in range(seats) if order[(place[s] + (k if side else -k)) % seats] < s]

    near = tuple(r for r in range(peers) if r < 2)
    far = tuple(r for r in range(peers) if r >= 2)

    first = step(prefix_key_values, prefix_key_values)
    chunks = split_columns([stretch_key_values, suffix_key_values], peers)
    chunks = [chunks[0]] + [across(chunks[r], r) for r in range(1, peers)]
    queries = split_columns([stretch_queries, suffix_queries], peers)
    own = [jnp.concatenate([c[i * tokens : (i + 1) * tokens] for c in chunks], axis=0) for i in range(2)]
    own, queries = lax.optimization_barrier((own, queries))
    queries = [queries[0]] + [across(queries[r], r) for r in range(1, peers)]

    pieces = [[(prefix_key_values, [(0, prefix_tokens, None)])] + [(p, [(0, prefix_tokens, None)]) for p in first]]
    cut = prefix_tokens // 2
    moving = jnp.concatenate([first[0], own[0]], axis=0), jnp.concatenate([own[0], first[1]], axis=0)
    for k in range(2, half + 1):
        count = prefix_tokens
        if k == half:
            count = cut
            moving = moving[0][cut:], moving[1][: seat_tokens + cut]
        moving = step(*moving)
        pieces.append(
            [
                (moving[0], [(0, count, None), (count, seat_tokens, seers(k - 1, 0))]),
                (moving[1], [(0, seat_tokens, seers(k - 1, 1)), (seat_tokens, count, None)]),
            ]
        )
    moving = step(moving[0][cut : cut + seat_tokens // 2], moving[1][seat_tokens // 2 : seat_tokens])
    pieces.append([(m, [(0, seat_tokens // 2, seers(half, side))]) for side, m in enumerate(moving)])
    pieces[-2:] = [pieces[-2] + pieces[-1]]

    def update(sets, piece, own=None, last=False):
        return attend(set_length, passage_first_slot, peers, sets, piece, own, last)

    near_set, far_set = (near, [queries[r] for r in near], None), (far, [queries[r] for r in far], None)
    (near_set,) = update([near_set], pieces[0], own)
    far_set = (far, lax.optimization_barrier((far_set[1], pieces[1][0][0]))[0], None)
    (far_set,) = update([far_set], pieces[0], own)
    for piece in pieces[1:-1]:
        near_set, far_set = update([near_set, far_set], piece)
    (far_out,) = update([far_set], pieces[-1], last=True)
    (near_out,) = update([near_set], pieces[-1], last=True)
    far_out = [across(c, r) for c, r in zip(far_out, far)]
    near_out = [across(c, r) if r else c for c, r in zip(near_out, near)]
    return tuple(join_columns(near_out + far_out, peers, tokens))


def solution(mesh):
    placed = (
        P(("seq", "head"), None),
        P(("seq", "head"), None),
        P(("seq", "head"), None),
        P(("seq", "head"), None),
        P("seq", "head"),
        P("seq"),
        P("seq", None),
    )
    return jax.shard_map(
        functools.partial(body, peers=mesh.shape["head"], seats=mesh.shape["seq"]),
        mesh=mesh,
        in_specs=placed,
        out_specs=(P(("seq", "head"), None), P(("seq", "head"), None)),
        check_vma=False,
    )
```

```python
import functools
import math

import jax
import jax.numpy as jnp
import numpy as np
from jax import lax
from jax.experimental import pallas as pl
from jax.experimental.pallas import tpu as pltpu
from jax.sharding import PartitionSpec as P

HEAD_SIZE = 128
GROUP = 8
PAIR = 2 * HEAD_SIZE
RATE = HEAD_SIZE ** (-0.5) * math.log2(math.e)
LOW = -1e30
PASSAGES = 4
AHEAD = 3
JOIN_VMEM = 8 * 1024 * 1024
VMEM_LIMIT = 40 * 1024 * 1024


def ring_order(count):
    wide = max(1, math.isqrt(count // 2))
    if count % wide or wide % 2 or wide < 2:
        return list(range(count))
    tall = count // wide
    order = [z * wide for z in range(tall)]
    for step, z in enumerate(reversed(range(tall))):
        row = [z * wide + x for x in range(1, wide)]
        order += row if step % 2 == 0 else row[::-1]
    return order


def is_one_of(index, members):
    found = jnp.int32(0)
    for base in range(0, max(members, default=0) + 1, 16):
        bits = sum(1 << (m - base) for m in members if base <= m < base + 16)
        found += jnp.where(index // 16 == base // 16, (jnp.int32(bits) >> (index % 16)) & 1, 0)
    return found > 0


def split_columns(arrays, peers):
    cols = arrays[0].shape[1] // peers
    me = lax.axis_index("head")
    return [
        jnp.concatenate([lax.dynamic_slice_in_dim(a, (me ^ r) * cols, cols, 1) for a in arrays], axis=0)
        for r in range(peers)
    ]


def join_columns(chunks, peers, rows):
    cols = chunks[0].shape[1]
    count = chunks[0].shape[0] // rows

    def kernel(*refs):
        ins, outs = refs[:peers], refs[peers : peers + count]
        me = lax.axis_index("head")
        copies = []
        for r in range(peers):
            start = pl.multiple_of((me ^ r) * cols, HEAD_SIZE)
            for o in range(count):
                source, target = ins[r].at[pl.ds(o * rows, rows)], outs[o].at[:, pl.ds(start, cols)]
                copies.append(pltpu.make_async_copy(source, target, refs[-1].at[r, o]))
        for copy in copies:
            copy.start()
        for copy in copies:
            copy.wait()

    return pl.pallas_call(
        kernel,
        out_shape=[jax.ShapeDtypeStruct((rows, cols * peers), chunks[0].dtype)] * count,
        in_specs=[pl.BlockSpec(memory_space=pltpu.VMEM)] * peers,
        out_specs=[pl.BlockSpec(memory_space=pl.ANY)] * count,
        scratch_shapes=[pltpu.SemaphoreType.DMA((peers, count))],
        compiler_params=pltpu.CompilerParams(vmem_limit_bytes=JOIN_VMEM),
        name="join_columns",
    )(*chunks)


def attend(length, starts, peers, sets, pieces, own, last):
    first = [state is None for _, _, state in sets]
    tokens = sets[0][1][0].shape[0] // 2 if first[0] else sets[0][1].shape[3] // (len(sets[0][0]) * GROUP)
    seat_tokens = peers * tokens
    heads = pieces[0][0].shape[1] // PAIR
    arrays = [p[0] for p in pieces] + list(own or ())
    spots = [(i,) + span for i, (_, spans) in enumerate(pieces) for span in spans]
    spots = [s for s in spots if s[3] is None] + [s for s in spots if s[3] is not None]
    n_prefix = sum(s[2] for s in spots if s[3] is None)
    n_common = sum(s[2] for s in spots)
    keys = n_common + (2 * seat_tokens if own else 0)

    flat = [length, starts] + arrays
    q_at, state_at = [], []
    for (ranks, queries, state), fresh in zip(sets, first):
        q_at.append(len(flat))
        flat += list(queries) if fresh else [queries]
        state_at.append(len(flat))
        flat += [] if fresh else list(state)

    mine = [len(ranks) * tokens for ranks, _, _ in sets]
    blocks = [GROUP * m for m in mine]
    out_shape, out_at = [], []
    for (ranks, _, _), fresh, block in zip(sets, first, blocks):
        out_at.append(len(out_shape))
        if last:
            out_shape += [jax.ShapeDtypeStruct((2 * tokens, heads * GROUP * HEAD_SIZE), jnp.bfloat16)] * len(ranks)
        else:
            out_shape.append(jax.ShapeDtypeStruct((heads, 2, HEAD_SIZE, block), jnp.float32))
            out_shape.append(jax.ShapeDtypeStruct((heads, 2, 8, block), jnp.float32))
            if fresh:
                out_shape.append(jax.ShapeDtypeStruct((heads, 2, HEAD_SIZE, block), jnp.bfloat16))

    def kernel(*refs):
        length_ref, starts_ref, array_refs = refs[0], refs[1], refs[2 : 2 + len(arrays)]
        in_refs, out_refs = refs[: len(flat)], refs[len(flat) : -2]
        k_ref, v_ref = refs[-2:]
        me = lax.axis_index("head")
        seat = lax.axis_index("seq")

        def query_positions(n, rows):
            index = lax.broadcasted_iota(jnp.int32, (rows, mine[n]), 1)
            rank = jnp.full_like(index, sets[n][0][0])
            for i, r in enumerate(sets[n][0][1:]):
                rank = jnp.where(index // tokens == i + 1, r, rank)
            return (me ^ rank) * tokens + index % tokens

        def tiled(allowed):
            return jnp.concatenate([jnp.where(allowed, 0.0, LOW)] * GROUP, axis=1)

        masks, live = [], []
        for n in range(len(sets)):
            if own:
                q_pos = query_positions(n, seat_tokens)
                index = lax.broadcasted_iota(jnp.int32, (seat_tokens, mine[n]), 0)
                k_pos = (me ^ (index // tokens)) * tokens + index % tokens
                before = k_pos <= q_pos
                q_set = k_set = jnp.zeros((seat_tokens, mine[n]), jnp.int32)
                for slot in range(PASSAGES):
                    q_set += (starts_ref[0, slot] <= q_pos).astype(jnp.int32)
                    k_set += (starts_ref[0, slot] <= k_pos).astype(jnp.int32)
                masks.append((tiled(before), tiled(before & (q_set == k_set) & (k_pos < length_ref[0]))))
            if last:
                live.append(tiled(query_positions(n, 1) < length_ref[0]) == 0.0)

        def load(h):
            base = h * PAIR

            def put(ref, low, count, top):
                k_ref[h, top : top + count, :] = ref[low : low + count, base : base + HEAD_SIZE]
                v_ref[h, :HEAD_SIZE, top : top + count] = jnp.transpose(
                    ref[low : low + count, base + HEAD_SIZE : base + PAIR]
                )

            top = 0
            for i, low, count, _ in spots:
                put(array_refs[i], low, count, top)
                top += count
            for ref in array_refs[len(pieces) :]:
                put(ref, 0, seat_tokens, top)
                top += seat_tokens
            v_ref[h, HEAD_SIZE:, :] = jnp.ones((16, keys), jnp.bfloat16)

        def look(n, h, kind):
            if first[n]:
                q = jnp.concatenate(
                    [
                        ref[kind * tokens : (kind + 1) * tokens, col * HEAD_SIZE : (col + 1) * HEAD_SIZE]
                        for col in range(h * GROUP, (h + 1) * GROUP)
                        for ref in in_refs[q_at[n] : state_at[n]]
                    ],
                    axis=0,
                )
                q = jnp.transpose(q)
                if not last:
                    out_refs[out_at[n] + 2][h, kind] = q
            else:
                q = in_refs[q_at[n]][h, kind]
            if kind == 0:
                spans = [(0, n_prefix, None)]
                top = n_prefix
                for _, _, count, seen in spots:
                    if seen is not None:
                        spans.append((top, top + count, is_one_of(seat, seen)))
                        top += count
                if own:
                    spans.append((n_common, n_common + seat_tokens, masks[n][0]))
            else:
                spans = [(0, n_common + (seat_tokens if own else 0), None)]
                if own:
                    spans.append((n_common + seat_tokens, n_common + 2 * seat_tokens, masks[n][1]))
            parts = []
            for low, high, allowed in spans:
                if low == high:
                    continue
                s = jnp.dot(k_ref[h, low:high, :], q, preferred_element_type=jnp.float32)
                if allowed is not None:
                    s = s + allowed if allowed.ndim == 2 else jnp.where(allowed, s, LOW)
                parts.append(s)
            return parts, functools.reduce(jnp.maximum, [jnp.max(s, axis=0, keepdims=True) for s in parts])

        def weigh(n, h, kind, parts, peak):
            if not first[n]:
                acc_ref, stats_ref = in_refs[state_at[n]], in_refs[state_at[n] + 1]
                old = stats_ref[h, kind, 0:1, :]
                peak = jnp.maximum(old, peak)
                fade = jnp.exp2((old - peak) * RATE)
            weights = jnp.concatenate([jnp.exp2((s - peak) * RATE).astype(jnp.bfloat16) for s in parts], axis=0)
            both = jnp.dot(v_ref[h, :, : weights.shape[0]], weights, preferred_element_type=jnp.float32)
            acc, total = both[:HEAD_SIZE], both[HEAD_SIZE : HEAD_SIZE + 1]
            if not first[n]:
                acc = acc + acc_ref[h, kind] * fade
                total = total + stats_ref[h, kind, 1:2, :] * fade
            if not last:
                out_refs[out_at[n]][h, kind] = acc
                out_refs[out_at[n] + 1][h, kind, 0:1, :] = peak
                out_refs[out_at[n] + 1][h, kind, 1:2, :] = total
                return
            result = acc * (1.0 / total)
            if kind == 1:
                result = jnp.where(live[n], result, 0.0)
            result = jnp.transpose(result.astype(jnp.bfloat16))
            for g in range(GROUP):
                col = (h * GROUP + g) * HEAD_SIZE
                for i in range(len(sets[n][0])):
                    row = g * mine[n] + i * tokens
                    out_refs[out_at[n] + i][kind * tokens : (kind + 1) * tokens, col : col + HEAD_SIZE] = result[
                        row : row + tokens
                    ]

        items = [(n, h, kind) for h in range(heads) for n in range(len(sets)) for kind in range(2)]
        for h in range(heads):
            load(h)
        queue = [look(*item) for item in items[:AHEAD]]
        for i, item in enumerate(items):
            if i + AHEAD < len(items):
                queue.append(look(*items[i + AHEAD]))
            weigh(*item, *queue[i])

    vmem = pl.BlockSpec(memory_space=pltpu.VMEM)
    rows = heads * 2 * sum(blocks)
    outs = pl.pallas_call(
        kernel,
        in_specs=[pl.BlockSpec(memory_space=pltpu.SMEM)] * 2 + [vmem] * (len(flat) - 2),
        out_specs=[vmem] * len(out_shape),
        out_shape=out_shape,
        scratch_shapes=[
            pltpu.VMEM((heads, keys, HEAD_SIZE), jnp.bfloat16),
            pltpu.VMEM((heads, HEAD_SIZE + 16, keys), jnp.bfloat16),
        ],
        compiler_params=pltpu.CompilerParams(vmem_limit_bytes=VMEM_LIMIT),
        cost_estimate=pl.CostEstimate(
            flops=rows * keys * HEAD_SIZE * 8, bytes_accessed=rows * HEAD_SIZE * 8, transcendentals=rows * keys
        ),
        name="attend",
    )(*flat)
    after = []
    for n, (ranks, queries, _) in enumerate(sets):
        got = outs[out_at[n] :]
        if last:
            after.append(got[: len(ranks)])
        else:
            after.append((ranks, got[2] if first[n] else queries, (got[0], got[1])))
    return after


def body(
    stretch_queries,
    stretch_key_values,
    suffix_queries,
    suffix_key_values,
    prefix_key_values,
    set_length,
    passage_first_slot,
    *,
    peers,
    seats,
):
    tokens = stretch_queries.shape[0]
    prefix_tokens = prefix_key_values.shape[0]
    seat_tokens = peers * tokens
    me = lax.axis_index("head").astype(jnp.int32)
    seat = lax.axis_index("seq").astype(jnp.int32)
    order = ring_order(seats)
    place = {s: i for i, s in enumerate(order)}
    right = [(order[i], order[(i + 1) % seats]) for i in range(seats)]
    left = [(b, a) for a, b in right]
    half = seats // 2

    def across(chunk, r):
        return lax.ppermute(chunk, "head", [(h, h ^ r) for h in range(peers)])

    def step(from_left, from_right):
        return lax.ppermute(from_left, "seq", right), lax.ppermute(from_right, "seq", left)

    def seers(k, side):
        return [s for s in range(seats) if order[(place[s] + (k if side else -k)) % seats] < s]

    near = tuple(r for r in range(peers) if r < 2)
    far = tuple(r for r in range(peers) if r >= 2)

    first = step(prefix_key_values, prefix_key_values)
    chunks = split_columns([stretch_key_values, suffix_key_values], peers)
    chunks = [chunks[0]] + [across(chunks[r], r) for r in range(1, peers)]
    queries = split_columns([stretch_queries, suffix_queries], peers)
    own = [jnp.concatenate([c[i * tokens : (i + 1) * tokens] for c in chunks], axis=0) for i in range(2)]
    own, queries = lax.optimization_barrier((own, queries))
    queries = [queries[0]] + [across(queries[r], r) for r in range(1, peers)]

    pieces = [[(prefix_key_values, [(0, prefix_tokens, None)])] + [(p, [(0, prefix_tokens, None)]) for p in first]]
    cut = prefix_tokens // 2
    moving = jnp.concatenate([first[0], own[0]], axis=0), jnp.concatenate([own[0], first[1]], axis=0)
    for k in range(2, half + 1):
        count = prefix_tokens
        if k == half:
            count = cut
            moving = moving[0][cut:], moving[1][: seat_tokens + cut]
        moving = step(*moving)
        pieces.append(
            [
                (moving[0], [(0, count, None), (count, seat_tokens, seers(k - 1, 0))]),
                (moving[1], [(0, seat_tokens, seers(k - 1, 1)), (seat_tokens, count, None)]),
            ]
        )
    moving = step(moving[0][cut : cut + seat_tokens // 2], moving[1][seat_tokens // 2 : seat_tokens])
    pieces.append([(m, [(0, seat_tokens // 2, seers(half, side))]) for side, m in enumerate(moving)])

    def update(sets, piece, own=None, last=False):
        return attend(set_length, passage_first_slot, peers, sets, piece, own, last)

    near_set, far_set = (near, [queries[r] for r in near], None), (far, [queries[r] for r in far], None)
    (near_set,) = update([near_set], pieces[0], own)
    far_set = (far, lax.optimization_barrier((far_set[1], pieces[1][0][0]))[0], None)
    (far_set,) = update([far_set], pieces[0], own)
    late = max(1, len(pieces) - 3)
    for piece in pieces[1:late]:
        near_set, far_set = update([near_set, far_set], piece)
    for piece in pieces[late:-2]:
        (far_set,) = update([far_set], piece)
    (far_out,) = update([far_set], pieces[-2] + pieces[-1], last=True)
    (near_out,) = update([near_set], [p for piece in pieces[late:] for p in piece], last=True)
    far_out = [across(c, r) for c, r in zip(far_out, far)]
    near_out = [across(c, r) if r else c for c, r in zip(near_out, near)]
    return tuple(join_columns(near_out + far_out, peers, tokens))


def solution(mesh):
    placed = (
        P(("seq", "head"), None),
        P(("seq", "head"), None),
        P(("seq", "head"), None),
        P(("seq", "head"), None),
        P("seq", "head"),
        P("seq"),
        P("seq", None),
    )
    return jax.shard_map(
        functools.partial(body, peers=mesh.shape["head"], seats=mesh.shape["seq"]),
        mesh=mesh,
        in_specs=placed,
        out_specs=(P(("seq", "head"), None), P(("seq", "head"), None)),
        check_vma=False,
    )
```

```python
import functools
import math

import jax
import jax.numpy as jnp
import numpy as np
from jax import lax
from jax.experimental import pallas as pl
from jax.experimental.pallas import tpu as pltpu
from jax.sharding import PartitionSpec as P

HEAD_SIZE = 128
GROUP = 8
PAIR = 2 * HEAD_SIZE
RATE = HEAD_SIZE ** (-0.5) * math.log2(math.e)
LOW = -1e30
PASSAGES = 4
AHEAD = 3
JOIN_VMEM = 8 * 1024 * 1024
VMEM_LIMIT = 40 * 1024 * 1024


def ring_order(count):
    wide = max(1, math.isqrt(count // 2))
    if count % wide or wide % 2 or wide < 2:
        return list(range(count))
    tall = count // wide
    order = [z * wide for z in range(tall)]
    for step, z in enumerate(reversed(range(tall))):
        row = [z * wide + x for x in range(1, wide)]
        order += row if step % 2 == 0 else row[::-1]
    return order


def is_one_of(index, members):
    found = jnp.int32(0)
    for base in range(0, max(members, default=0) + 1, 16):
        bits = sum(1 << (m - base) for m in members if base <= m < base + 16)
        found += jnp.where(index // 16 == base // 16, (jnp.int32(bits) >> (index % 16)) & 1, 0)
    return found > 0


def split_columns(arrays, peers):
    cols = arrays[0].shape[1] // peers
    me = lax.axis_index("head")
    return [
        jnp.concatenate([lax.dynamic_slice_in_dim(a, (me ^ r) * cols, cols, 1) for a in arrays], axis=0)
        for r in range(peers)
    ]


def join_columns(chunks, peers, rows):
    cols = chunks[0].shape[1]
    count = chunks[0].shape[0] // rows

    def kernel(*refs):
        ins, outs = refs[:peers], refs[peers : peers + count]
        me = lax.axis_index("head")
        copies = []
        for r in range(peers):
            start = pl.multiple_of((me ^ r) * cols, HEAD_SIZE)
            for o in range(count):
                source, target = ins[r].at[pl.ds(o * rows, rows)], outs[o].at[:, pl.ds(start, cols)]
                copies.append(pltpu.make_async_copy(source, target, refs[-1].at[r, o]))
        for copy in copies:
            copy.start()
        for copy in copies:
            copy.wait()

    return pl.pallas_call(
        kernel,
        out_shape=[jax.ShapeDtypeStruct((rows, cols * peers), chunks[0].dtype)] * count,
        in_specs=[pl.BlockSpec(memory_space=pltpu.VMEM)] * peers,
        out_specs=[pl.BlockSpec(memory_space=pl.ANY)] * count,
        scratch_shapes=[pltpu.SemaphoreType.DMA((peers, count))],
        compiler_params=pltpu.CompilerParams(vmem_limit_bytes=JOIN_VMEM),
        name="join_columns",
    )(*chunks)


def attend(length, starts, peers, sets, pieces, own, last):
    first = [state is None for _, _, state in sets]
    tokens = sets[0][1][0].shape[0] // 2 if first[0] else sets[0][1].shape[3] // (len(sets[0][0]) * GROUP)
    seat_tokens = peers * tokens
    heads = pieces[0][0].shape[1] // PAIR
    arrays = [p[0] for p in pieces] + list(own or ())
    spots = [(i,) + span for i, (_, spans) in enumerate(pieces) for span in spans]
    spots = [s for s in spots if s[3] is None] + [s for s in spots if s[3] is not None]
    n_prefix = sum(s[2] for s in spots if s[3] is None)
    n_common = sum(s[2] for s in spots)
    keys = n_common + (2 * seat_tokens if own else 0)

    flat = [length, starts] + arrays
    q_at, state_at = [], []
    for (ranks, queries, state), fresh in zip(sets, first):
        q_at.append(len(flat))
        flat += list(queries) if fresh else [queries]
        state_at.append(len(flat))
        flat += [] if fresh else list(state)

    mine = [len(ranks) * tokens for ranks, _, _ in sets]
    blocks = [GROUP * m for m in mine]
    out_shape, out_at = [], []
    for (ranks, _, _), fresh, block in zip(sets, first, blocks):
        out_at.append(len(out_shape))
        if last:
            out_shape += [jax.ShapeDtypeStruct((2 * tokens, heads * GROUP * HEAD_SIZE), jnp.bfloat16)] * len(ranks)
        else:
            out_shape.append(jax.ShapeDtypeStruct((heads, 2, HEAD_SIZE, block), jnp.float32))
            out_shape.append(jax.ShapeDtypeStruct((heads, 2, 8, block), jnp.float32))
            if fresh:
                out_shape.append(jax.ShapeDtypeStruct((heads, 2, HEAD_SIZE, block), jnp.bfloat16))

    def kernel(*refs):
        length_ref, starts_ref, array_refs = refs[0], refs[1], refs[2 : 2 + len(arrays)]
        in_refs, out_refs = refs[: len(flat)], refs[len(flat) : -2]
        k_ref, v_ref = refs[-2:]
        me = lax.axis_index("head")
        seat = lax.axis_index("seq")

        def query_positions(n, rows):
            index = lax.broadcasted_iota(jnp.int32, (rows, mine[n]), 1)
            rank = jnp.full_like(index, sets[n][0][0])
            for i, r in enumerate(sets[n][0][1:]):
                rank = jnp.where(index // tokens == i + 1, r, rank)
            return (me ^ rank) * tokens + index % tokens

        def tiled(allowed):
            return jnp.concatenate([jnp.where(allowed, 0.0, LOW)] * GROUP, axis=1)

        masks, live = [], []
        for n in range(len(sets)):
            if own:
                q_pos = query_positions(n, seat_tokens)
                index = lax.broadcasted_iota(jnp.int32, (seat_tokens, mine[n]), 0)
                k_pos = (me ^ (index // tokens)) * tokens + index % tokens
                before = k_pos <= q_pos
                q_set = k_set = jnp.zeros((seat_tokens, mine[n]), jnp.int32)
                for slot in range(PASSAGES):
                    q_set += (starts_ref[0, slot] <= q_pos).astype(jnp.int32)
                    k_set += (starts_ref[0, slot] <= k_pos).astype(jnp.int32)
                masks.append((tiled(before), tiled(before & (q_set == k_set) & (k_pos < length_ref[0]))))
            if last:
                live.append(tiled(query_positions(n, 1) < length_ref[0]) == 0.0)

        def load(h):
            base = h * PAIR

            def put(ref, low, count, top):
                k_ref[h, top : top + count, :] = ref[low : low + count, base : base + HEAD_SIZE]
                v_ref[h, :HEAD_SIZE, top : top + count] = jnp.transpose(
                    ref[low : low + count, base + HEAD_SIZE : base + PAIR]
                )

            top = 0
            for i, low, count, _ in spots:
                put(array_refs[i], low, count, top)
                top += count
            for ref in array_refs[len(pieces) :]:
                put(ref, 0, seat_tokens, top)
                top += seat_tokens
            v_ref[h, HEAD_SIZE:, :] = jnp.ones((16, keys), jnp.bfloat16)

        def look(n, h, kind):
            if first[n]:
                q = jnp.concatenate(
                    [
                        ref[kind * tokens : (kind + 1) * tokens, col * HEAD_SIZE : (col + 1) * HEAD_SIZE]
                        for col in range(h * GROUP, (h + 1) * GROUP)
                        for ref in in_refs[q_at[n] : state_at[n]]
                    ],
                    axis=0,
                )
                q = jnp.transpose(q)
                if not last:
                    out_refs[out_at[n] + 2][h, kind] = q
            else:
                q = in_refs[q_at[n]][h, kind]
            if kind == 0:
                spans = [(0, n_prefix, None)]
                top = n_prefix
                for _, _, count, seen in spots:
                    if seen is not None:
                        spans.append((top, top + count, is_one_of(seat, seen)))
                        top += count
                if own:
                    spans.append((n_common, n_common + seat_tokens, masks[n][0]))
            else:
                spans = [(0, n_common + (seat_tokens if own else 0), None)]
                if own:
                    spans.append((n_common + seat_tokens, n_common + 2 * seat_tokens, masks[n][1]))
            parts = []
            for low, high, allowed in spans:
                if low == high:
                    continue
                s = jnp.dot(k_ref[h, low:high, :], q, preferred_element_type=jnp.float32)
                if allowed is not None:
                    s = s + allowed if allowed.ndim == 2 else jnp.where(allowed, s, LOW)
                parts.append(s)
            return parts, functools.reduce(jnp.maximum, [jnp.max(s, axis=0, keepdims=True) for s in parts])

        def weigh(n, h, kind, parts, peak):
            if not first[n]:
                acc_ref, stats_ref = in_refs[state_at[n]], in_refs[state_at[n] + 1]
                old = stats_ref[h, kind, 0:1, :]
                peak = jnp.maximum(old, peak)
                fade = jnp.exp2((old - peak) * RATE)
            weights = jnp.concatenate([jnp.exp2((s - peak) * RATE).astype(jnp.bfloat16) for s in parts], axis=0)
            both = jnp.dot(v_ref[h, :, : weights.shape[0]], weights, preferred_element_type=jnp.float32)
            acc, total = both[:HEAD_SIZE], both[HEAD_SIZE : HEAD_SIZE + 1]
            if not first[n]:
                acc = acc + acc_ref[h, kind] * fade
                total = total + stats_ref[h, kind, 1:2, :] * fade
            if not last:
                out_refs[out_at[n]][h, kind] = acc
                out_refs[out_at[n] + 1][h, kind, 0:1, :] = peak
                out_refs[out_at[n] + 1][h, kind, 1:2, :] = total
                return
            result = acc * (1.0 / total)
            if kind == 1:
                result = jnp.where(live[n], result, 0.0)
            result = jnp.transpose(result.astype(jnp.bfloat16))
            for g in range(GROUP):
                col = (h * GROUP + g) * HEAD_SIZE
                for i in range(len(sets[n][0])):
                    row = g * mine[n] + i * tokens
                    out_refs[out_at[n] + i][kind * tokens : (kind + 1) * tokens, col : col + HEAD_SIZE] = result[
                        row : row + tokens
                    ]

        items = [(n, h, kind) for h in range(heads) for n in range(len(sets)) for kind in range(2)]
        for h in range(heads):
            load(h)
        queue = [look(*item) for item in items[:AHEAD]]
        for i, item in enumerate(items):
            if i + AHEAD < len(items):
                queue.append(look(*items[i + AHEAD]))
            weigh(*item, *queue[i])

    vmem = pl.BlockSpec(memory_space=pltpu.VMEM)
    rows = heads * 2 * sum(blocks)
    outs = pl.pallas_call(
        kernel,
        in_specs=[pl.BlockSpec(memory_space=pltpu.SMEM)] * 2 + [vmem] * (len(flat) - 2),
        out_specs=[vmem] * len(out_shape),
        out_shape=out_shape,
        scratch_shapes=[
            pltpu.VMEM((heads, keys, HEAD_SIZE), jnp.bfloat16),
            pltpu.VMEM((heads, HEAD_SIZE + 16, keys), jnp.bfloat16),
        ],
        compiler_params=pltpu.CompilerParams(vmem_limit_bytes=VMEM_LIMIT),
        cost_estimate=pl.CostEstimate(
            flops=rows * keys * HEAD_SIZE * 8, bytes_accessed=rows * HEAD_SIZE * 8, transcendentals=rows * keys
        ),
        name="attend",
    )(*flat)
    after = []
    for n, (ranks, queries, _) in enumerate(sets):
        got = outs[out_at[n] :]
        if last:
            after.append(got[: len(ranks)])
        else:
            after.append((ranks, got[2] if first[n] else queries, (got[0], got[1])))
    return after


def body(
    stretch_queries,
    stretch_key_values,
    suffix_queries,
    suffix_key_values,
    prefix_key_values,
    set_length,
    passage_first_slot,
    *,
    peers,
    seats,
):
    tokens = stretch_queries.shape[0]
    prefix_tokens = prefix_key_values.shape[0]
    seat_tokens = peers * tokens
    me = lax.axis_index("head").astype(jnp.int32)
    seat = lax.axis_index("seq").astype(jnp.int32)
    order = ring_order(seats)
    place = {s: i for i, s in enumerate(order)}
    right = [(order[i], order[(i + 1) % seats]) for i in range(seats)]
    left = [(b, a) for a, b in right]
    half = seats // 2

    def across(chunk, r):
        return lax.ppermute(chunk, "head", [(h, h ^ r) for h in range(peers)])

    def step(from_left, from_right):
        return lax.ppermute(from_left, "seq", right), lax.ppermute(from_right, "seq", left)

    def seers(k, side):
        return [s for s in range(seats) if order[(place[s] + (k if side else -k)) % seats] < s]

    near = tuple(r for r in range(peers) if r < 2)
    far = tuple(r for r in range(peers) if r >= 2)

    first = step(prefix_key_values, prefix_key_values)
    chunks = split_columns([stretch_key_values, suffix_key_values], peers)
    chunks = [chunks[0]] + [across(chunks[r], r) for r in range(1, peers)]
    queries = split_columns([stretch_queries, suffix_queries], peers)
    own = [jnp.concatenate([c[i * tokens : (i + 1) * tokens] for c in chunks], axis=0) for i in range(2)]
    own, queries = lax.optimization_barrier((own, queries))
    queries = [queries[0]] + [across(queries[r], r) for r in range(1, peers)]

    near_by = step(own[0], own[0])
    pieces = [[(prefix_key_values, [(0, prefix_tokens, None)])] + [(p, [(0, prefix_tokens, None)]) for p in first]]
    pieces[0] += [(p, [(0, seat_tokens, seers(1, side))]) for side, p in enumerate(near_by)]
    moving = [jnp.concatenate([p, q], axis=0) for p, q in zip(first, near_by)]
    def update(sets, piece, own=None, last=False):
        return attend(set_length, passage_first_slot, peers, sets, piece, own, last)

    near_set, far_set = (near, [queries[r] for r in near], None), (far, [queries[r] for r in far], None)
    (near_set,) = update([near_set], pieces[0], own)
    for k in range(2, half + 1):
        spans = [[(0, prefix_tokens, None), (prefix_tokens, seat_tokens, seers(k, side))] for side in range(2)]
        if k == half:
            cut = prefix_tokens // 2 + seat_tokens // 2
            moving = moving[0][:cut], moving[1][cut:]
            spans[0] = [(0, cut, None)]
            spans[1] = [(0, prefix_tokens - cut, None), (prefix_tokens - cut, seat_tokens, seers(k, 1))]
        moving = step(*moving)
        if k == 2:
            moving, near_queries = lax.optimization_barrier((moving, near_set[1]))
            near_set = (near, near_queries, near_set[2])
        pieces.append(list(zip(moving, spans)))

    far_set = (far, lax.optimization_barrier((far_set[1], pieces[1][0][0]))[0], None)
    (far_set,) = update([far_set], pieces[0], own)
    late = max(1, len(pieces) - 2)
    for piece in pieces[1:late]:
        near_set, far_set = update([near_set, far_set], piece)
    for piece in pieces[late:-1]:
        (far_set,) = update([far_set], piece)
    (far_out,) = update([far_set], pieces[-1], last=True)
    (near_out,) = update([near_set], [p for piece in pieces[late:] for p in piece], last=True)
    far_out = [across(c, r) for c, r in zip(far_out, far)]
    near_out = [across(c, r) if r else c for c, r in zip(near_out, near)]
    return tuple(join_columns(near_out + far_out, peers, tokens))


def solution(mesh):
    placed = (
        P(("seq", "head"), None),
        P(("seq", "head"), None),
        P(("seq", "head"), None),
        P(("seq", "head"), None),
        P("seq", "head"),
        P("seq"),
        P("seq", None),
    )
    return jax.shard_map(
        functools.partial(body, peers=mesh.shape["head"], seats=mesh.shape["seq"]),
        mesh=mesh,
        in_specs=placed,
        out_specs=(P(("seq", "head"), None), P(("seq", "head"), None)),
        check_vma=False,
    )
```
